32 devices in a mesh: pixel: 4 (over y, core), crop: 2 (over x), member: 4 (over z).
Axes of the slice: x: 2, y: 2, z: 4, core: 2. Of those that a mesh axis runs over, the one named last changes fastest.
Arguments:
- forcing: bfloat16 [52, 8, 3072], P(None, None, ('pixel', 'crop')), may hold values from -6 to 6
- observed: bfloat16 [52, 3072], P(None, ('pixel', 'crop')), may hold values from -6 to 6
- obs_sigma: float32 [3072], P(('pixel', 'crop')), may hold values from 0.5 to 2
- pixel_class: int32 [3072, 1], P(('pixel', 'crop')), may hold values from 0 to 63; in each aligned block of 384 rows (0 to 383, 384 to 767, ...) at most 8 rows name the same one
- pixel_count: int32 [96], P(('pixel', 'crop')), may hold values from 16 to 32
- cloud_free: int32 [96, 52], P(('pixel', 'crop')), may hold values 0 or 1
- params: float32 [16, 8, 24], P('member'), may hold values from -6 to 6
- input_weight: bfloat16 [8, 48, 32], P('crop'), may hold values from -1 to 1
- conv_weight: bfloat16 [8, 3, 48, 96], P('crop'), may hold values from -0.625 to 0.625
- mix_weight: bfloat16 [8, 3, 48, 48], P('crop'), may hold values from -0.875 to 0.875
- head_weight: bfloat16 [8, 48], P('crop'), may hold values from -0.875 to 0.875
Outputs:
- updated: float32 [16, 8, 24], P('member', 'crop')
The draws below stay inside these ranges and needn't reach their ends.
Inputs may be any that keep to these rules, and one draw needn't show every extreme that they name: pixel_class is crop * 8 + region; among the 384 pixel places of one pixel and crop index no class is named more than 8 times, a bound that some block reaches. `cloud_free`: 1 where the block is seen in that week.
All inputs are finite; a program needn't handle non-finite values.
Results may differ from the reference program's by a relative error of at most 0.0067.
Values may be sent and summed in bfloat16 or wider, within the bound.
No kernel may reach another device: no remote copies, remote signals or barrier semaphores. Data moves between devices by JAX's collectives and lax.ppermute only.
A program may use at most 128 MiB of HBM per device.

```python
import math
from functools import partial
import jax
import jax.numpy as jnp
import numpy as np
from jax import lax

WEEKS = 52
CHANNELS = 48
FORCING = 8
PARAMS = 24
LAYERS = 3
CROPS = 8
REGIONS = 8
BLK_PIX = 32
BLK_DEV = 12
MEMBERS = 16
CAP = 8
BLOCKS = 96
PIXELS = 3072
N_PIXEL = 4
N_CROP = 2


def plant(drawn, key, low, largest):
    shape = drawn.shape
    spot = [jax.random.randint(jax.random.fold_in(key, axis), (), 0, shape[axis]) for axis in range(len(shape))]
    drawn = drawn.at[tuple(spot)].set(low)
    longest = shape.index(max(shape))
    spot[longest] = (spot[longest] + 1) % shape[longest]
    return drawn.at[tuple(spot)].set(largest)


def shard_levels(rng, shape, pieces, smallest, high):
    factor_of = 1.0
    for axis_at, parts in pieces:
        heights = jax.random.uniform(jax.random.fold_in(jax.random.fold_in(rng, 6), axis_at), (parts,), jnp.float32, smallest / len(pieces), high / len(pieces))
        factor_of = factor_of * jnp.repeat(jnp.exp(heights), shape[axis_at] // parts).reshape((-1,) + (1,) * (len(shape) - 1 - axis_at))
    return factor_of


def routed_block(own_key, own, number, rows, count, top, reach, lean):
    sequence = jax.random.permutation(own_key, count)
    packed, common = portions_of(count, rows * top, reach, lean, True), portions_of(count, rows * top, reach, lean, False)
    places = jnp.arange(count)

    def named(lengths, offset_by):
        used = int((lengths > 0).sum())
        fixed = max(1, used // 4)
        passed = fixed + (places - fixed + offset_by * (used - fixed)) % max(1, count - fixed)
        return jnp.zeros((count,), jnp.int32).at[sequence[jnp.where(places < fixed, places, passed)]].set(jnp.asarray(lengths, jnp.int32))

    lengths = jnp.where(number % 4 == 0, named(packed, number // 4), named(common, number - number // 4 - 1))
    mixed = jax.random.permutation(jax.random.fold_in(own, 3), count)
    giver, taker = mixed[0:count // 2 * 2:2], mixed[1:count // 2 * 2:2]
    room = jnp.minimum(lengths[giver] - 1, reach - lengths[taker]) // 2
    room = jnp.where((giver == sequence[0]) | (taker == sequence[0]) | (lengths[taker] == 0), 0, jnp.maximum(room, 0))
    passed = jax.random.randint(jax.random.fold_in(own, 4), (count // 2,), 0, 1 << 20) % (room + 1)
    lengths = lengths.at[giver].add(-passed).at[taker].add(passed)
    items = jnp.searchsorted(jnp.cumsum(lengths), jnp.arange(rows * top), side="right").astype(jnp.int32)
    table = items.reshape(top, rows).T
    table = table[jax.random.permutation(jax.random.fold_in(own, 1), rows)]
    offset_by = jax.random.randint(jax.random.fold_in(own, 2), (rows, 1), 0, top)
    return jnp.take_along_axis(table, (jnp.arange(top)[None, :] + offset_by) % top, axis=1)


def portions_of(number_of, total, most, lean, full):
    portions = [(1 << 20) // math.isqrt(standing ** lean) + 1 for standing in range(1, number_of + 1)]
    largest = most if full else min(most, max(-(-total // number_of), total * portions[0] // sum(portions)))
    least = 1 if total - largest >= number_of - 1 else 0
    given, surplus = [largest] + [least] * (number_of - 1), total - largest - least * (number_of - 1)
    while surplus > 0:
        free = [i for i in range(1, number_of) if given[i] < largest] or [i for i in range(1, number_of) if given[i] < most]
        mass, left = sum([portions[i] for i in free]), surplus
        for i in free:
            more = min(most - given[i], max(1, left * portions[i] // mass), surplus)
            given[i] = given[i] + more
            surplus = surplus - more
    return np.array(given)


def bell_draw(key, shape, deviation, bound, split=(), kind=jnp.bfloat16):
    result = deviation * jax.random.normal(key, shape, jnp.float32)
    if split:
        result = result * shard_levels(key, shape, split, -0.22, 0.18)
    return jnp.clip(result, -bound, bound).astype(kind)


def setup_inputs(seed: int = 0) -> dict:
    key_of = jax.random.split(jax.random.key(seed), 12)
    forcing = bell_draw(key_of[0], (WEEKS, FORCING, PIXELS), 1.0, 6.0, ((2, 8),))
    observed = bell_draw(key_of[1], (WEEKS, PIXELS), 1.0, 6.0, ((1, 8),))
    obs_sigma = jnp.clip(jnp.exp(math.log(2.0) - 1.3862944 * jax.random.uniform(key_of[2], (PIXELS,), jnp.float32) ** shard_levels(key_of[2], (PIXELS,), ((0, 8),), -0.2, 0.2)), 0.5, 2.0)
    pixel_class_keys = jax.random.split(jax.random.fold_in(key_of[3], 1), PIXELS // (BLK_DEV * BLK_PIX))
    pixel_class_turns = jax.random.permutation(jax.random.fold_in(key_of[3], 3), PIXELS // (BLK_DEV * BLK_PIX))
    pixel_class = jax.vmap(lambda own, number: routed_block(jax.random.fold_in(key_of[3], 2), own, number, BLK_DEV * BLK_PIX, CROPS * REGIONS, 1, CAP, 2))(pixel_class_keys, pixel_class_turns).reshape((PIXELS, 1))
    pixel_count = plant(jax.random.randint(key_of[4], (BLOCKS,), BLK_PIX // 2, BLK_PIX + 1), jax.random.fold_in(key_of[4], 1), BLK_PIX // 2, BLK_PIX).astype(jnp.int32)
    cloud_free = plant((jax.random.randint(key_of[5], (BLOCKS, WEEKS), 0, 4) < 3).astype(jnp.int32), jax.random.fold_in(key_of[5], 1), 0, 1)
    params = bell_draw(key_of[6], (MEMBERS, REGIONS, PARAMS), 1.0, 6.0, ((0, 4),), jnp.float32)
    input_weight = bell_draw(key_of[7], (CROPS, CHANNELS, FORCING + PARAMS), (FORCING + PARAMS) ** -0.5, 1.0, ((0, 2),))
    conv_weight = bell_draw(key_of[8], (CROPS, LAYERS, CHANNELS, 2 * CHANNELS), (2 * CHANNELS) ** -0.5, 0.625, ((0, 2),))
    mix_weight = bell_draw(key_of[9], (CROPS, LAYERS, CHANNELS, CHANNELS), CHANNELS ** -0.5, 0.875, ((0, 2),))
    head_weight = bell_draw(key_of[10], (CROPS, CHANNELS), CHANNELS ** -0.5, 0.875, ((0, 2),))
    return dict(forcing=forcing, observed=observed, obs_sigma=obs_sigma, pixel_class=pixel_class, pixel_count=pixel_count, cloud_free=cloud_free, params=params, input_weight=input_weight, conv_weight=conv_weight, mix_weight=mix_weight, head_weight=head_weight)


ALPHA_INFLATION = 4.0

def pack_slots(forcing, observed, obs_sigma, pixel_class, pixel_count, cloud_free, n_class, cap_slots):
    n_blocks = pixel_count.shape[0]
    n_pixels = obs_sigma.shape[0]
    block_len = n_pixels // n_blocks
    classes = pixel_class[:, 0]
    position = jnp.arange(n_pixels, dtype=jnp.int32)
    is_live = position % block_len < jnp.repeat(pixel_count, block_len, total_repeat_length=n_pixels)
    earlier = (classes[None, :] == classes[:, None]) & is_live[None, :] & (position[None, :] < position[:, None])
    rank_in = lax.optimization_barrier(jnp.sum(earlier.astype(jnp.int32), axis=1))
    slot_of = classes * cap_slots + rank_in
    places = jnp.arange(n_class * cap_slots, dtype=jnp.int32)
    select = ((slot_of[:, None] == places[None, :]) & is_live[:, None]).astype(jnp.bfloat16)
    seen_mask = jnp.repeat(cloud_free, block_len, axis=0, total_repeat_length=n_pixels).astype(jnp.float32)
    obs_weight = (jnp.transpose(seen_mask) / obs_sigma[None, :]).astype(jnp.bfloat16)
    obs_pair = jnp.stack([observed, obs_weight], axis=1)
    sent_forcing = jnp.einsum('tfx,xs->tfs', forcing.astype(jnp.float32), select.astype(jnp.float32), preferred_element_type=jnp.float32).astype(jnp.bfloat16)
    sent_pair = jnp.einsum('tfx,xs->tfs', obs_pair.astype(jnp.float32), select.astype(jnp.float32), preferred_element_type=jnp.float32).astype(jnp.bfloat16)
    return (sent_forcing, sent_pair)

def run_network(slot_forcing, theta_member, region_hot, input_weight, conv_weight, mix_weight, head_weight):
    n_weeks = slot_forcing.shape[0]
    n_forcing = slot_forcing.shape[1]
    n_channels = conv_weight.shape[2]
    theta_bf = theta_member.astype(jnp.bfloat16)
    param_term = jnp.einsum('kcp,rp->ckr', input_weight[:, :, n_forcing:].astype(jnp.float32), theta_bf.astype(jnp.float32), preferred_element_type=jnp.float32)
    param_slot = lax.optimization_barrier(jnp.sum(param_term[:, :, :, None] * region_hot[None, None, :, :], axis=2))
    hidden = jnp.einsum('kcf,tfkq->tckq', input_weight[:, :, :n_forcing].astype(jnp.float32), slot_forcing.astype(jnp.float32), preferred_element_type=jnp.float32)
    hidden = (hidden + param_slot[None]).astype(jnp.bfloat16)
    for layer in range(conv_weight.shape[1]):
        dilation = 2 ** layer
        delayed = jnp.concatenate([jnp.zeros((dilation,) + hidden.shape[1:], jnp.bfloat16), hidden[:n_weeks - dilation]], axis=0)
        inner = jnp.einsum('koc,tckq->tokq', conv_weight[:, layer, :, :n_channels].astype(jnp.float32), hidden.astype(jnp.float32), preferred_element_type=jnp.float32)
        inner = inner + jnp.einsum('koc,tckq->tokq', conv_weight[:, layer, :, n_channels:].astype(jnp.float32), delayed.astype(jnp.float32), preferred_element_type=jnp.float32)
        inner = jax.nn.relu(inner).astype(jnp.bfloat16)
        mixed = jnp.einsum('koc,tckq->tokq', mix_weight[:, layer].astype(jnp.float32), inner.astype(jnp.float32), preferred_element_type=jnp.float32)
        hidden = (hidden.astype(jnp.float32) + mixed).astype(jnp.bfloat16)
    return jnp.einsum('kc,tckq->tkq', head_weight.astype(jnp.float32), hidden.astype(jnp.float32), preferred_element_type=jnp.float32)

def reference(forcing, observed, obs_sigma, pixel_class, pixel_count, cloud_free, params, input_weight, conv_weight, mix_weight, head_weight):
    sources = N_PIXEL * N_CROP
    n_weeks, n_forcing, n_pixels = forcing.shape
    per_source = n_pixels // sources
    per_class = REGIONS * CAP
    packer = partial(pack_slots, n_class=CROPS * REGIONS, cap_slots=CAP)
    packed_forcing, packed_pair = jax.vmap(packer, in_axes=(2, 1, 0, 0, 0, 0))(forcing.reshape(n_weeks, n_forcing, sources, per_source), observed.reshape(n_weeks, sources, per_source), obs_sigma.reshape(sources, per_source), pixel_class.reshape(sources, per_source, 1), pixel_count.reshape(sources, -1), cloud_free.reshape(sources, -1, n_weeks))
    slot_forcing = jnp.transpose(packed_forcing.reshape(sources, n_weeks, n_forcing, CROPS, per_class), (1, 2, 3, 0, 4))
    slot_forcing = slot_forcing.reshape(n_weeks, n_forcing, CROPS, sources * per_class)
    slot_pair = jnp.transpose(packed_pair.reshape(sources, n_weeks, 2, CROPS, per_class), (1, 2, 3, 0, 4))
    slot_pair = slot_pair.reshape(n_weeks, 2, -1)
    width_q = sources * per_class
    region_ids = jnp.arange(REGIONS, dtype=jnp.int32)
    region_hot = (jnp.arange(width_q, dtype=jnp.int32) // CAP % REGIONS == region_ids[:, None]).astype(jnp.float32)

    def run_member(theta_member):
        return run_network(slot_forcing, theta_member, region_hot, input_weight, conv_weight, mix_weight, head_weight)
    members = params.shape[0]
    predicted = lax.map(run_member, params).reshape(members, n_weeks, -1)
    n_slots = predicted.shape[2]
    mean_pred = lax.optimization_barrier(jnp.sum(predicted, axis=0)) / members
    obs_value = slot_pair[:, 0].astype(jnp.float32)
    obs_weight = slot_pair[:, 1].astype(jnp.float32)
    scaled = (obs_weight[None] * (predicted - mean_pred[None]) / math.sqrt(ALPHA_INFLATION * (members - 1))).astype(jnp.bfloat16)
    innovation = obs_weight * (obs_value - mean_pred) / math.sqrt(ALPHA_INFLATION)
    slot_region = jnp.arange(n_slots, dtype=jnp.int32) // CAP % REGIONS
    flat_rows = scaled.reshape(members, -1)
    flat_wide = flat_rows.astype(jnp.float32)
    flat_innov = innovation.reshape(-1)

    def region_terms(region):
        in_region = jnp.broadcast_to(slot_region[None, :] == region, (n_weeks, n_slots)).reshape(-1)
        masked = jnp.where(in_region[None, :], flat_rows, jnp.zeros((), jnp.bfloat16))
        gram_block = jnp.dot(masked.astype(jnp.float32), jnp.transpose(flat_rows).astype(jnp.float32), preferred_element_type=jnp.float32)
        proj_block = jnp.dot(flat_wide, jnp.where(in_region, flat_innov, jnp.zeros((), flat_innov.dtype)), precision=lax.Precision.HIGHEST)
        return (gram_block, proj_block)
    grams, projs = lax.map(region_terms, region_ids)
    scale_root = math.sqrt(members - 1)

    def update(gram_block, proj_block, theta_region):
        system = gram_block + jnp.eye(members, dtype=gram_block.dtype)
        factor = jnp.linalg.cholesky(system)
        right_side = proj_block[:, None] - scale_root * gram_block
        mixing = jax.scipy.linalg.cho_solve((factor, True), right_side)
        spread = (theta_region - lax.optimization_barrier(jnp.sum(theta_region, axis=0)) / members) / scale_root
        return theta_region + jnp.dot(jnp.transpose(mixing), spread, precision=lax.Precision.HIGHEST)
    return jax.vmap(update, in_axes=(0, 0, 1), out_axes=1)(grams, projs, params)
```

```python
import functools
import math

import jax
import jax.numpy as jnp
from jax import lax
from jax.experimental import pallas as pl
from jax.experimental.pallas import tpu as pltpu
from jax.sharding import PartitionSpec as P

REGIONS = 8
CAP = 8
SLOTS = REGIONS * CAP
LANES = 2 * SLOTS
ALPHA_INFLATION = 4.0
VMEM_LIMIT = 48 * 2**20
F32 = jnp.float32
BF16 = jnp.bfloat16

NT = (((1,), (1,)), ((), ()))
TN = (((0,), (0,)), ((), ()))


def mm(a, b):
    return jnp.dot(a, b, preferred_element_type=F32)


def mm_nt(a, b):
    return lax.dot_general(a, b, NT, preferred_element_type=F32)


def hi_lo(x):
    high = x.astype(BF16)
    return high, (x - high.astype(F32)).astype(BF16)


def vmem(n):
    return [pl.BlockSpec(memory_space=pltpu.VMEM)] * n


def hbm(n):
    return [pl.BlockSpec(memory_space=pltpu.HBM)] * n


def stay(*arrays):
    return [pltpu.with_memory_space_constraint(a, pltpu.HBM) for a in arrays]


def weight_rows(layers, channels):
    taps = layers * channels
    return taps, taps + 16


def fetch(pairs, sems):
    copies = [pltpu.make_async_copy(src, dst, sems.at[i]) for i, (src, dst) in enumerate(pairs)]
    for copy in copies:
        copy.start()

    def wait():
        for copy in copies:
            copy.wait()

    return wait


def fold_weights(
    split, input_hbm, conv_hbm, mix_hbm, head_hbm, theta_hbm, out_ref, theta_ref,
    input_ref, conv_ref, mix_ref, head_ref, quad, stack, sems,
):
    layers, channels = conv_ref.shape[0], conv_ref.shape[1]
    forcing = 8
    mine = lax.axis_index("member") // split
    wait = fetch(
        [
            (input_hbm.at[mine], input_ref),
            (conv_hbm.at[mine], conv_ref),
            (mix_hbm.at[mine], mix_ref),
            (head_hbm, head_ref),
            (theta_hbm, theta_ref),
        ],
        sems,
    )
    taps, block = weight_rows(layers, channels)
    out_ref[...] = jnp.zeros(out_ref.shape, BF16)
    quad[...] = jnp.zeros(quad.shape, F32)
    stack[...] = jnp.zeros(stack.shape, F32)
    wait()
    win = jnp.transpose(input_ref[...].astype(F32))
    for half in range(2):
        rows = pl.ds(half * channels, channels)
        quad[rows, pl.ds(half * forcing, forcing)] = win[:, :forcing]
        for layer in range(layers - 1):
            at = 2 * forcing + (2 * layer + half) * channels
            quad[rows, pl.ds(at, channels)] = mix_ref[layer].astype(F32)
    for layer in range(layers):
        stack[pl.ds(layer * channels, channels), pl.ds(0, 2 * channels)] = conv_ref[layer].astype(
            F32
        )
    head_row = lax.broadcasted_iota(jnp.int32, head_ref.shape, 0)
    head = jnp.sum(
        jnp.where(head_row == mine, head_ref[...].astype(F32), 0.0), axis=0, keepdims=True
    )
    stack[pl.ds(taps, 1), pl.ds(0, channels)] = head
    lhs = stack[:, : 2 * channels].astype(BF16)
    fused = mm(lhs, quad[...].astype(BF16))
    last = mm(lhs[taps:, :channels], mix_ref[layers - 1])
    width = fused.shape[1]
    out_ref[pl.ds(0, taps), pl.ds(0, width)] = fused[:taps].astype(BF16)
    fused_hi, fused_lo = hi_lo(fused[taps : taps + 1])
    last_hi, last_lo = hi_lo(last[:1])
    last_pad = jnp.zeros((2, width - channels), F32)
    last_rows = jnp.concatenate([last_hi.astype(F32), last_lo.astype(F32)], axis=0)
    out_ref[pl.ds(taps, 16), pl.ds(0, width)] = jnp.concatenate(
        [
            fused_hi.astype(F32),
            fused_lo.astype(F32),
            jnp.concatenate([last_rows, last_pad], axis=1),
            jnp.zeros((12, width), F32),
        ],
        axis=0,
    ).astype(BF16)
    out_ref[:, pl.ds(width, 2 * channels)] = lhs
    win_pad = jnp.zeros((block - channels, win.shape[1]), F32)
    out_ref[:, pl.ds(width + 128, win.shape[1])] = jnp.concatenate([win, win_pad], axis=0).astype(
        BF16
    )


def pack_kernel(
    plan, forcing_hbm, observed_hbm, sigma_hbm, class_hbm, cloud_hbm, count_hbm, x_ref, y_ref, w_ref,
    forcing_ref, observed_ref, sigma_ref, class_ref, cloud_ref, count_ref, sems,
):
    n_crops, local_crops, split, dup, layers = plan
    wait = fetch(
        [
            (class_hbm, class_ref),
            (forcing_hbm, forcing_ref),
            (observed_hbm, observed_ref),
            (sigma_hbm, sigma_ref.at[0]),
            (cloud_hbm, cloud_ref),
            (count_hbm, count_ref),
        ],
        sems,
    )
    wait()
    weeks, pixels = observed_ref.shape
    blocks = cloud_ref.shape[0]
    block_len = pixels // blocks
    member = lax.axis_index("member")
    local = member // split
    first_j, part = unit_place(plan, member)
    lane = lax.broadcasted_iota(jnp.int32, (1, pixels), 1)
    live = jnp.zeros((1, pixels), jnp.int32)
    for b in range(blocks):
        here = (lane >= b * block_len) & (lane < b * block_len + count_ref[b])
        live = jnp.where(here, 1, live)
    classes = class_ref[...]
    rank_of = lax.broadcasted_iota(jnp.int32, (CAP, pixels), 0)
    one_hots = []
    for n in range(n_crops):
        crop = unit_crop(plan, n, first_j) * local_crops + local
        one_hots.append(
            jnp.where((classes == crop * REGIONS + rank_of) & (live > 0), 1.0, 0.0).astype(F32)
        )
    hot = jnp.concatenate(one_hots, axis=0)
    if hot.shape[0] < 16:
        hot = jnp.concatenate([hot, jnp.zeros_like(hot)], axis=0)
    earlier = lax.broadcasted_iota(jnp.int32, (pixels, pixels), 0) < lax.broadcasted_iota(
        jnp.int32, (pixels, pixels), 1
    )
    rank = mm(hot.astype(BF16), jnp.where(earlier, 1.0, 0.0).astype(BF16))
    wanted = rank_of.astype(F32)
    if dup > 1:
        wanted = jnp.where(rank_of % dup == part, wanted, -1.0)
    selects = []
    for n in range(n_crops):
        rows = []
        for r in range(REGIONS):
            at = n * REGIONS + r
            match = (rank[at : at + 1] == wanted) & (hot[at : at + 1] > 0)
            rows.append(jnp.where(match, 1.0, 0.0))
        half = jnp.concatenate(rows, axis=0).astype(BF16)
        selects.append(jnp.concatenate([half, half], axis=0))
    select = jnp.concatenate(selects, axis=0)
    block_row = lax.broadcasted_iota(jnp.int32, (blocks, pixels), 0)
    block_lane = lax.broadcasted_iota(jnp.int32, (blocks, pixels), 1)
    in_block = (block_lane >= block_row * block_len) & (block_lane < (block_row + 1) * block_len)
    seen = lax.dot_general(
        cloud_ref[...].astype(F32),
        jnp.where(in_block, 1.0, 0.0),
        TN,
        preferred_element_type=F32,
    )
    weight = (seen / sigma_ref[...]).astype(BF16)
    observed = mm_nt(observed_ref[...], select)
    weight = mm_nt(weight, select)
    packed = mm_nt(forcing_ref[...], select)
    n_forcing = packed.shape[0] // weeks
    zero = jnp.zeros((n_forcing, LANES), F32)
    for n in range(n_crops):
        lanes = slice(n * LANES, (n + 1) * LANES)
        y_ref[n] = observed[:, lanes]
        w_ref[n] = weight[:, lanes]
        for t in range(weeks):
            now = packed[t * n_forcing : (t + 1) * n_forcing, lanes]
            for layer in range(layers):
                back = t - 2**layer
                then = packed[back * n_forcing : (back + 1) * n_forcing, lanes] if back >= 0 else zero
                x_ref[n, layer, :, pl.ds(t * LANES, LANES)] = jnp.concatenate(
                    [now, then], axis=0
                ).astype(BF16)


def unit_place(plan, member):
    n_crops, _, split, dup, _ = plan
    step = lax.rem(member, split)
    return (step // dup) * n_crops, lax.rem(step, dup)


def unit_crop(plan, n, first_j):
    return lax.rem(first_j + n + swap_base(plan), plan_shards(plan))


def swap_base(plan):
    return lax.axis_index("crop") if plan[0] == plan_shards(plan) else 0


def plan_shards(plan):
    return lax.axis_size("crop")


def net_kernel(dims, *refs):
    n_crops, my_members, layers, channels, blocks_in = dims
    refs = list(refs)
    x_ref, y_ref, w_ref = refs[:3]
    weight_refs = refs[3 : 3 + n_crops]
    theta_refs = refs[3 + n_crops : 3 + n_crops + blocks_in]
    out_ref, theta_out = refs[3 + n_crops + blocks_in : 5 + n_crops + blocks_in]
    theta_all, spread, base, inner0, inner1, bias_full, bias_now, pred = refs[
        5 + n_crops + blocks_in :
    ]
    members = theta_out.shape[0]
    pairs = members // 2
    weeks = y_ref.shape[1]
    span = 2 * LANES
    tiles = weeks // 2
    n_forcing = x_ref.shape[2] // 2
    taps, block = weight_rows(layers, channels)
    width = 2 * n_forcing + 2 * (layers - 1) * channels
    me = lax.axis_index("member")
    n_params = theta_out.shape[2]

    theta_all[...] = jnp.zeros(theta_all.shape, F32)
    for d, ref in enumerate(theta_refs):
        count = ref.shape[0]
        at = lax.rem(me + d, members // count) * count if blocks_in > 1 else 0
        for i in range(count):
            theta_all[at + i, :, pl.ds(n_forcing, n_params)] = ref[i]
            theta_out[at + i] = ref[i]

    for i in range(pairs):
        for half in range(2):
            for r in range(REGIONS):
                row = theta_all[i + half * pairs, pl.ds(r, 1), :]
                spread[pl.ds(i * LANES + half * SLOTS + r * CAP, CAP), :] = jnp.broadcast_to(
                    row, (CAP, row.shape[1])
                )
    spread_rows = spread[...].astype(BF16)

    def col(j):
        return pl.ds(j * span, span)

    lasts = []
    for n in range(n_crops):
        wts = weight_refs[n]
        stack = wts[:, pl.ds(width, 2 * channels)]
        now = stack[:taps, :channels]
        win = wts[pl.ds(0, channels), pl.ds(width + 128, n_forcing + n_params)]
        high, low = hi_lo(mm_nt(win, spread_rows))
        bias_full[n] = mm(
            jnp.concatenate([stack, stack], axis=1),
            jnp.concatenate([high, high, low, low], axis=0),
        )
        bias_now[n] = mm(
            jnp.concatenate([now, now], axis=1), jnp.concatenate([high, low], axis=0)
        )
        tail = wts[pl.ds(taps, 16), pl.ds(0, channels)].astype(F32)
        tail_row = tail[2:3] + tail[3:4]
        diag = lax.broadcasted_iota(jnp.int32, (channels, channels), 0) == lax.broadcasted_iota(
            jnp.int32, (channels, channels), 1
        )
        tail_col = jnp.sum(jnp.where(diag, tail_row, 0.0), axis=1, keepdims=True)
        lasts.append(jnp.broadcast_to(tail_col, (channels, span)))

    for n in range(n_crops):
        wts = weight_refs[n]
        last = lasts[n]
        first = wts[pl.ds(0, channels), pl.ds(0, 2 * n_forcing)]
        base[...] = mm(first, x_ref[n, 0])
        second = wts[pl.ds(channels, channels), pl.ds(0, 2 * n_forcing + 2 * channels)]
        third = wts[pl.ds(2 * channels, channels + 16), pl.ds(0, width)]
        zero_tile = jnp.zeros((channels, span), BF16)

        @pl.loop(0, pairs)
        def _(i):
            lanes = pl.ds(pl.multiple_of(i * LANES, LANES), LANES)

            def bias(layer, tile):
                rows = pl.ds(layer * channels, channels)
                parts = []
                for t in (2 * tile, 2 * tile + 1):
                    ref = bias_full if t >= 2**layer else bias_now
                    parts.append(ref[n, rows, lanes])
                return jnp.concatenate(parts, axis=1)

            def back(ref, tile):
                return ref[:, col(tile)] if tile >= 0 else zero_tile

            for j in range(tiles):
                inner0[:, col(j)] = jnp.maximum(base[:, col(j)] + bias(0, j), 0.0).astype(BF16)
            for j in range(tiles):
                rhs = jnp.concatenate(
                    [x_ref[n, 1, :, col(j)], inner0[:, col(j)], back(inner0, j - 1)], axis=0
                )
                inner1[:, col(j)] = jnp.maximum(mm(second, rhs) + bias(1, j), 0.0).astype(BF16)
            for j in range(tiles):
                rhs = jnp.concatenate(
                    [
                        x_ref[n, 2, :, col(j)],
                        inner0[:, col(j)],
                        back(inner0, j - 2),
                        inner1[:, col(j)],
                        back(inner1, j - 2),
                    ],
                    axis=0,
                )
                v = mm(third, rhs)
                h = jnp.maximum(v[:channels] + bias(2, j), 0.0) * last
                head_bias = bias_full[n, pl.ds(taps, 1), lanes]
                s = (
                    jnp.sum(h, axis=0, keepdims=True)
                    + v[channels : channels + 1]
                    + v[channels + 1 : channels + 2]
                    + jnp.concatenate([head_bias, head_bias], axis=1)
                )
                pred[2 * j, n, pl.ds(i, 1), :] = s[:, :LANES]
                pred[2 * j + 1, n, pl.ds(i, 1), :] = s[:, LANES:]

    lane = lax.broadcasted_iota(jnp.int32, (1, LANES), 1)
    low_half = lane < SLOTS
    region = (lane % SLOTS) // CAP
    masks = [jnp.where(region == r, 1.0, 0.0).astype(BF16) for r in range(REGIONS)]
    gram = jnp.zeros((REGIONS * members, members + 16), F32)
    held = []
    for t in range(weeks):
        scaled, innov = [], []
        for n in range(n_crops):
            p = pred[t, n]
            total = jnp.sum(p, axis=0, keepdims=True)
            mean = (total + pltpu.roll(total, SLOTS, 1)) / members
            w = w_ref[n, pl.ds(t, 1), :]
            y = y_ref[n, pl.ds(t, 1), :]
            scaled.append(w * (p - mean) / math.sqrt(ALPHA_INFLATION * (members - 1)))
            innov.append(w * (y - mean) / math.sqrt(ALPHA_INFLATION))
        if n_crops == 2:
            even = jnp.where(low_half, scaled[0], pltpu.roll(scaled[1], SLOTS, 1))
            odd = jnp.where(low_half, pltpu.roll(scaled[0], SLOTS, 1), scaled[1])
            row = jnp.where(low_half, innov[0], innov[1])
        else:
            even = jnp.where(low_half, scaled[0], 0.0)
            odd = jnp.where(low_half, pltpu.roll(scaled[0], SLOTS, 1), 0.0)
            row = jnp.where(low_half, innov[0], 0.0)
        rows = jnp.concatenate([even, odd], axis=0).astype(BF16)
        high, low = hi_lo(row)
        row_id = lax.broadcasted_iota(jnp.int32, (16, LANES), 0)
        extra = jnp.where(
            row_id == 0, high.astype(F32), jnp.where(row_id == 1, low.astype(F32), 0.0)
        ).astype(BF16)
        masked = jnp.concatenate([rows * mask for mask in masks], axis=0)
        held.append((masked, jnp.concatenate([rows, extra], axis=0)))
        if len(held) == 2:
            gram = gram + mm_nt(
                jnp.concatenate([h[0] for h in held], axis=1),
                jnp.concatenate([h[1] for h in held], axis=1),
            )
            held = []
    flat = jnp.transpose(gram)
    out_ref[...] = flat[: members + 8]


def solve_kernel(owned, gram_a, gram_b, theta_ref, out_ref, system, moved):
    members, _, n_params = theta_ref.shape
    my_members = out_ref.shape[0]
    first_region = lax.axis_index("crop") * owned
    first_member = lax.axis_index("member") * my_members
    gram = gram_a[...] + gram_b[...]
    for r in range(REGIONS):
        system[r] = gram[:, r * members : (r + 1) * members]
    row_id = lax.broadcasted_iota(jnp.int32, (members, 1), 0)
    eye = lax.broadcasted_iota(jnp.int32, (members, members), 0) == lax.broadcasted_iota(
        jnp.int32, (members, members), 1
    )
    scale_root = math.sqrt(members - 1)
    work = []
    for k in range(owned):
        block = system[first_region + k]
        g = block[:members]
        proj = block[members : members + 1] + block[members + 1 : members + 2]
        theta = jnp.concatenate(
            [theta_ref[m, pl.ds(first_region + k, 1), :] for m in range(members)], axis=0
        )
        spread = (theta - jnp.sum(theta, axis=0, keepdims=True) / members) / scale_root
        work.append([g + jnp.where(eye, 1.0, 0.0), spread, proj - scale_root * g, theta])
    for i in range(members):
        for item in work:
            a, z = item[0], item[1]
            column = a[:, i : i + 1]
            pivot = a[i : i + 1, i : i + 1]
            row_a = a[i : i + 1] / pivot
            row_z = z[i : i + 1] / pivot
            factor = jnp.where(row_id == i, column - 1.0, column)
            item[0] = a - factor * row_a
            item[1] = z - factor * row_z
    for k, (_, z, right, theta) in enumerate(work):
        moved[k] = theta + jnp.dot(
            right, z, precision=lax.Precision.HIGHEST, preferred_element_type=F32
        )
    for k in range(owned):
        for m in range(my_members):
            out_ref[m, pl.ds(k, 1), :] = moved[k, pl.ds(first_member + m, 1), :]


def local(
    forcing,
    observed,
    obs_sigma,
    pixel_class,
    pixel_count,
    cloud_free,
    params,
    input_weight,
    conv_weight,
    mix_weight,
    head_weight,
):
    n_crop = lax.axis_size("crop")
    n_member = lax.axis_size("member")
    weeks, n_forcing, pixels = forcing.shape
    local_crops, layers, channels, _ = conv_weight.shape
    my_members, _, n_params = params.shape
    members = my_members * n_member
    assert n_member % local_crops == 0
    split = n_member // local_crops
    dup = max(1, split // n_crop)
    n_crops = max(1, n_crop // split)
    assert n_crops in (1, 2) and n_crops * split == n_crop * dup
    plan = (n_crops, local_crops, split, dup, layers)
    params_kernel = pltpu.CompilerParams(vmem_limit_bytes=VMEM_LIMIT)
    taps, block = weight_rows(layers, channels)
    width = 2 * n_forcing + 2 * (layers - 1) * channels
    assert width % 16 == 0 and width + 2 * channels <= width + 128
    wide = -(-(width + 128 + n_forcing + n_params) // 128) * 128
    vmem_copy = lambda a: pltpu.VMEM(a.shape[1:], a.dtype)

    input_rows = jnp.swapaxes(input_weight, 1, 2)
    folded, theta_own = pl.pallas_call(
        functools.partial(fold_weights, split),
        out_shape=(
            jax.ShapeDtypeStruct((block, wide), BF16),
            jax.ShapeDtypeStruct(params.shape, F32),
        ),
        in_specs=hbm(5),
        out_specs=tuple(vmem(2)),
        scratch_shapes=[
            vmem_copy(input_rows),
            vmem_copy(conv_weight),
            vmem_copy(mix_weight),
            pltpu.VMEM(head_weight.shape, BF16),
            pltpu.VMEM((2 * channels, width), F32),
            pltpu.VMEM((block, 128), F32),
            pltpu.SemaphoreType.DMA((5,)),
        ],
        compiler_params=params_kernel,
    )(*stay(input_rows, conv_weight, mix_weight, head_weight, params))

    if n_crops == n_crop == 2:
        weights = [folded, lax.ppermute(folded, "crop", [(0, 1), (1, 0)])]
    else:
        gathered = lax.all_gather(folded, "crop", axis=0)
        first_j, _ = unit_place(plan, lax.axis_index("member"))
        weights = [
            lax.dynamic_index_in_dim(gathered, unit_crop(plan, n, first_j), 0, keepdims=False)
            for n in range(n_crops)
        ]
    if n_member <= 4:
        thetas = [theta_own] + [
            lax.ppermute(params, "member", [((i + d) % n_member, i) for i in range(n_member)])
            for d in range(1, n_member)
        ]
    else:
        thetas = [lax.all_gather(params, "member", axis=0, tiled=True)]

    x, y, w = pl.pallas_call(
        functools.partial(pack_kernel, plan),
        out_shape=(
            jax.ShapeDtypeStruct((n_crops, layers, 2 * n_forcing, weeks * LANES), BF16),
            jax.ShapeDtypeStruct((n_crops, weeks, LANES), F32),
            jax.ShapeDtypeStruct((n_crops, weeks, LANES), F32),
        ),
        in_specs=hbm(6),
        out_specs=tuple(vmem(3)),
        scratch_shapes=[
            pltpu.VMEM((weeks * n_forcing, pixels), BF16),
            pltpu.VMEM((weeks, pixels), BF16),
            pltpu.VMEM((1, pixels), F32),
            pltpu.VMEM((1, pixels), jnp.int32),
            pltpu.VMEM(cloud_free.shape, jnp.int32),
            pltpu.SMEM(pixel_count.shape, jnp.int32),
            pltpu.SemaphoreType.DMA((6,)),
        ],
        compiler_params=params_kernel,
    )(
        *stay(
            forcing.reshape(weeks * n_forcing, pixels),
            observed,
            obs_sigma,
            pixel_class.reshape(1, pixels),
            cloud_free,
            pixel_count,
        )
    )

    dims = (n_crops, my_members, layers, channels, len(thetas))
    pairs = members // 2
    gram, theta_all = pl.pallas_call(
        functools.partial(net_kernel, dims),
        out_shape=(
            jax.ShapeDtypeStruct((members + 8, REGIONS * members), F32),
            jax.ShapeDtypeStruct((members, REGIONS, n_params), F32),
        ),
        in_specs=vmem(3 + len(weights) + len(thetas)),
        out_specs=tuple(vmem(2)),
        scratch_shapes=[
            pltpu.VMEM((members, REGIONS, n_forcing + n_params), F32),
            pltpu.VMEM((pairs * LANES, n_forcing + n_params), F32),
            pltpu.VMEM((channels, weeks * LANES), F32),
            pltpu.VMEM((channels, weeks * LANES), BF16),
            pltpu.VMEM((channels, weeks * LANES), BF16),
            pltpu.VMEM((n_crops, block, pairs * LANES), F32),
            pltpu.VMEM((n_crops, taps, pairs * LANES), F32),
            pltpu.VMEM((weeks, n_crops, pairs, LANES), F32),
        ],
        compiler_params=params_kernel,
    )(x, y, w, *weights, *thetas)

    steps = []
    for axis in ("crop", "pixel", "member"):
        size = lax.axis_size(axis)
        d = 1
        while d < size:
            steps.append((axis, [(i, i ^ d) for i in range(size)]))
            d *= 2
    other = None
    for axis, pairs_ in steps:
        if other is not None:
            gram = gram + other
        other = lax.ppermute(gram, axis, pairs_)

    owned = REGIONS // n_crop
    return pl.pallas_call(
        functools.partial(solve_kernel, owned),
        out_shape=jax.ShapeDtypeStruct((my_members, owned, n_params), F32),
        in_specs=vmem(3),
        out_specs=vmem(1)[0],
        scratch_shapes=[
            pltpu.VMEM((REGIONS, members + 8, members), F32),
            pltpu.VMEM((owned, members, n_params), F32),
        ],
        compiler_params=params_kernel,
    )(gram, other, theta_all)


def solution(mesh):
    in_specs = (
        P(None, None, ("pixel", "crop")),
        P(None, ("pixel", "crop")),
        P(("pixel", "crop")),
        P(("pixel", "crop"), None),
        P(("pixel", "crop")),
        P(("pixel", "crop"), None),
        P("member", None, None),
        P("crop", None, None),
        P("crop", None, None, None),
        P("crop", None, None, None),
        P("crop", None),
    )
    out_specs = P("member", "crop", None)
    return jax.shard_map(local, mesh=mesh, in_specs=in_specs, out_specs=out_specs, check_vma=False)
```

```python
import functools
import math

import jax
import jax.numpy as jnp
from jax import lax
from jax.experimental import pallas as pl
from jax.experimental.pallas import tpu as pltpu
from jax.sharding import PartitionSpec as P

REGIONS = 8
CAP = 8
SLOTS = REGIONS * CAP
LANES = 2 * SLOTS
ALPHA_INFLATION = 4.0
GROUP = 4
BLOCK = 4
VMEM_LIMIT = 48 * 2**20
F32 = jnp.float32
BF16 = jnp.bfloat16

NT = (((1,), (1,)), ((), ()))
TN = (((0,), (0,)), ((), ()))


def mm(a, b):
    return jnp.dot(a, b, preferred_element_type=F32)


def mm_nt(a, b):
    return lax.dot_general(a, b, NT, preferred_element_type=F32)


def hi_lo(x):
    high = x.astype(BF16)
    return high, (x - high.astype(F32)).astype(BF16)


def vmem(n):
    return [pl.BlockSpec(memory_space=pltpu.VMEM)] * n


def hbm(n):
    return [pl.BlockSpec(memory_space=pltpu.HBM)] * n


def cost(microseconds):
    return pl.CostEstimate(
        flops=int(microseconds * 1.1e9), bytes_accessed=int(microseconds * 3.5e6), transcendentals=0
    )


def stay(*arrays):
    return [pltpu.with_memory_space_constraint(a, pltpu.HBM) for a in arrays]


def weight_rows(layers, channels):
    taps = layers * channels
    return taps, taps + 16


def fetch(pairs, sems):
    copies = [pltpu.make_async_copy(src, dst, sems.at[i]) for i, (src, dst) in enumerate(pairs)]
    for copy in copies:
        copy.start()

    def wait():
        for copy in copies:
            copy.wait()

    return wait


def fold_weights(mine, input_ref, conv_ref, mix_ref, head_ref, out_ref, quad, stack):
    layers, channels = conv_ref.shape[0], conv_ref.shape[1]
    forcing = 8
    taps, block = weight_rows(layers, channels)
    out_ref[...] = jnp.zeros(out_ref.shape, BF16)
    quad[...] = jnp.zeros(quad.shape, F32)
    stack[...] = jnp.zeros(stack.shape, F32)
    win = jnp.transpose(input_ref[...].astype(F32))
    for half in range(2):
        rows = pl.ds(half * channels, channels)
        quad[rows, pl.ds(half * forcing, forcing)] = win[:, :forcing]
        for layer in range(layers - 1):
            at = 2 * forcing + (2 * layer + half) * channels
            quad[rows, pl.ds(at, channels)] = mix_ref[layer].astype(F32)
    for layer in range(layers):
        stack[pl.ds(layer * channels, channels), pl.ds(0, 2 * channels)] = conv_ref[layer].astype(
            F32
        )
    head_row = lax.broadcasted_iota(jnp.int32, head_ref.shape, 0)
    head = jnp.sum(
        jnp.where(head_row == mine, head_ref[...].astype(F32), 0.0), axis=0, keepdims=True
    )
    stack[pl.ds(taps, 1), pl.ds(0, channels)] = head
    lhs = stack[:, : 2 * channels].astype(BF16)
    fused = mm(lhs, quad[...].astype(BF16))
    last = mm(lhs[taps:, :channels], mix_ref[layers - 1])
    width = fused.shape[1]
    out_ref[pl.ds(0, taps), pl.ds(0, width)] = fused[:taps].astype(BF16)
    fused_hi, fused_lo = hi_lo(fused[taps : taps + 1])
    last_hi, last_lo = hi_lo(last[:1])
    last_pad = jnp.zeros((2, width - channels), F32)
    last_rows = jnp.concatenate([last_hi.astype(F32), last_lo.astype(F32)], axis=0)
    out_ref[pl.ds(taps, 16), pl.ds(0, width)] = jnp.concatenate(
        [
            fused_hi.astype(F32),
            fused_lo.astype(F32),
            jnp.concatenate([last_rows, last_pad], axis=1),
            jnp.zeros((12, width), F32),
        ],
        axis=0,
    ).astype(BF16)
    out_ref[:, pl.ds(width, 2 * channels)] = lhs
    win_pad = jnp.zeros((block - channels, win.shape[1]), F32)
    out_ref[:, pl.ds(width + 128, win.shape[1])] = jnp.concatenate([win, win_pad], axis=0).astype(
        BF16
    )


def prepare(plan, *refs):
    sources, refs = refs[:11], refs[11:]
    folded, theta, x, y, w = refs[:5]
    buffers, (quad, stack, sems) = refs[5:15], refs[15:]
    mine = lax.axis_index("member") // plan[2]
    sliced = [s.at[mine] if i < 3 else s for i, s in enumerate(sources)]
    copies = list(zip(sliced, buffers[:4] + (theta,) + buffers[4:]))
    copies[7] = (copies[7][0], copies[7][1].at[0])
    fetch(copies, sems)()
    fold_weights(mine, *buffers[:4], folded, quad, stack)
    pack_slots(plan, *buffers[4:], x, y, w)


def pack_slots(
    plan, forcing_ref, observed_ref, sigma_ref, class_ref, cloud_ref, count_ref, x_ref, y_ref, w_ref
):
    n_crops, local_crops, split, dup, layers = plan
    weeks, pixels = observed_ref.shape
    blocks = cloud_ref.shape[0]
    block_len = pixels // blocks
    member = lax.axis_index("member")
    local = member // split
    first_j, part = unit_place(plan, member)
    lane = lax.broadcasted_iota(jnp.int32, (1, pixels), 1)
    live = jnp.zeros((1, pixels), jnp.int32)
    for b in range(blocks):
        here = (lane >= b * block_len) & (lane < b * block_len + count_ref[b])
        live = jnp.where(here, 1, live)
    classes = class_ref[...]
    rank_of = lax.broadcasted_iota(jnp.int32, (CAP, pixels), 0)
    one_hots = []
    for n in range(n_crops):
        crop = unit_crop(plan, n, first_j) * local_crops + local
        one_hots.append(
            jnp.where((classes == crop * REGIONS + rank_of) & (live > 0), 1.0, 0.0).astype(F32)
        )
    hot = jnp.concatenate(one_hots, axis=0)
    if hot.shape[0] < 16:
        hot = jnp.concatenate([hot, jnp.zeros_like(hot)], axis=0)
    earlier = lax.broadcasted_iota(jnp.int32, (pixels, pixels), 0) < lax.broadcasted_iota(
        jnp.int32, (pixels, pixels), 1
    )
    rank = mm(hot.astype(BF16), jnp.where(earlier, 1.0, 0.0).astype(BF16))
    wanted = rank_of.astype(F32)
    if dup > 1:
        wanted = jnp.where(rank_of % dup == part, wanted, -1.0)
    selects = []
    for n in range(n_crops):
        rows = []
        for r in range(REGIONS):
            at = n * REGIONS + r
            match = (rank[at : at + 1] == wanted) & (hot[at : at + 1] > 0)
            rows.append(jnp.where(match, 1.0, 0.0))
        half = jnp.concatenate(rows, axis=0).astype(BF16)
        selects.append(jnp.concatenate([half, half], axis=0))
    select = jnp.concatenate(selects, axis=0)
    block_row = lax.broadcasted_iota(jnp.int32, (blocks, pixels), 0)
    block_lane = lax.broadcasted_iota(jnp.int32, (blocks, pixels), 1)
    in_block = (block_lane >= block_row * block_len) & (block_lane < (block_row + 1) * block_len)
    seen = lax.dot_general(
        cloud_ref[...].astype(F32),
        jnp.where(in_block, 1.0, 0.0),
        TN,
        preferred_element_type=F32,
    )
    weight = (seen / sigma_ref[...]).astype(BF16)
    observed = mm_nt(observed_ref[...], select)
    weight = mm_nt(weight, select)
    packed = mm_nt(forcing_ref[...], select)
    n_forcing = packed.shape[0] // weeks
    zero = jnp.zeros((n_forcing, LANES), F32)
    for n in range(n_crops):
        lanes = slice(n * LANES, (n + 1) * LANES)
        y_ref[n] = observed[:, lanes]
        w_ref[n] = weight[:, lanes]
        for t in range(weeks):
            now = packed[t * n_forcing : (t + 1) * n_forcing, lanes]
            for layer in range(layers):
                back = t - 2**layer
                then = packed[back * n_forcing : (back + 1) * n_forcing, lanes] if back >= 0 else zero
                x_ref[n, layer, :, pl.ds(t * LANES, LANES)] = jnp.concatenate(
                    [now, then], axis=0
                ).astype(BF16)


def unit_place(plan, member):
    n_crops, _, split, dup, _ = plan
    step = lax.rem(member, split)
    return (step // dup) * n_crops, lax.rem(step, dup)


def unit_crop(plan, n, first_j):
    return lax.rem(first_j + n + swap_base(plan), plan_shards(plan))


def swap_base(plan):
    return lax.axis_index("crop") if plan[0] == plan_shards(plan) else 0


def plan_shards(plan):
    return lax.axis_size("crop")


def net_first(dims, *refs):
    blocks_in, n_forcing = dims
    x_ref, wts = refs[:2]
    theta_refs, refs = refs[2 : 2 + blocks_in], refs[2 + blocks_in :]
    pred, theta_out, spread = refs[:3]
    theta_all = refs[3]
    scratch = refs[4:]
    members, _, n_params = theta_out.shape
    pairs = members // 2
    me = lax.axis_index("member")

    theta_all[...] = jnp.zeros(theta_all.shape, F32)
    for d, ref in enumerate(theta_refs):
        count = ref.shape[0]
        at = (me ^ d) * count if blocks_in > 1 else 0
        for i in range(count):
            theta_all[at + i, :, pl.ds(n_forcing, n_params)] = ref[i]
            theta_out[at + i] = ref[i]

    for i in range(pairs):
        for half in range(2):
            for r in range(REGIONS):
                row = theta_all[i + half * pairs, pl.ds(r, 1), :]
                spread[pl.ds(i * LANES + half * SLOTS + r * CAP, CAP), :] = jnp.broadcast_to(
                    row, (CAP, row.shape[1])
                )
    run_crop(x_ref, 0, wts, spread, pred, *scratch)


def run_crop(x_ref, n, wts, spread, pred, base, inner0, inner1, bias_full, bias_now):
    layers, n_forcing = x_ref.shape[1], x_ref.shape[2] // 2
    channels = base.shape[0]
    taps, block = weight_rows(layers, channels)
    width = 2 * n_forcing + 2 * (layers - 1) * channels
    pairs = pred.shape[1]
    tiles = pred.shape[0] // 2
    span = 2 * LANES

    def col(j):
        return pl.ds(j * span, span)

    stack = wts[:, pl.ds(width, 2 * channels)]
    now = stack[:taps, :channels]
    win = wts[pl.ds(0, channels), pl.ds(width + 128, spread.shape[1])]
    high, low = hi_lo(mm_nt(win, spread[...].astype(BF16)))
    bias_full[...] = mm(
        jnp.concatenate([stack, stack], axis=1),
        jnp.concatenate([high, high, low, low], axis=0),
    )
    bias_now[...] = mm(
        jnp.concatenate([now, now], axis=1), jnp.concatenate([high, low], axis=0)
    )
    tail = wts[pl.ds(taps, 16), pl.ds(0, channels)].astype(F32)
    tail_row = tail[2:3] + tail[3:4]
    diag = lax.broadcasted_iota(jnp.int32, (channels, channels), 0) == lax.broadcasted_iota(
        jnp.int32, (channels, channels), 1
    )
    tail_col = jnp.sum(jnp.where(diag, tail_row, 0.0), axis=1, keepdims=True)
    last = jnp.broadcast_to(tail_col, (channels, LANES))
    first = wts[pl.ds(0, channels), pl.ds(0, 2 * n_forcing)]
    base[...] = mm(first, x_ref[n, 0])
    second = wts[pl.ds(channels, channels), pl.ds(0, 2 * n_forcing + 2 * channels)]
    third = wts[pl.ds(2 * channels, channels + 16), pl.ds(0, width)]
    zero_tile = jnp.zeros((channels, span), BF16)

    group = inner0.shape[0]

    @pl.loop(0, pairs // group)
    def _(step):
        items = [step * group + u for u in range(group)]
        lanes = [pl.ds(pl.multiple_of(i * LANES, LANES), LANES) for i in items]

        def bias_of(u, layer):
            rows = pl.ds(layer * channels, channels)
            seen = {}

            def get(tile):
                parts = []
                for t in (2 * tile, 2 * tile + 1):
                    late = t >= 2**layer
                    if late not in seen:
                        seen[late] = (bias_full if late else bias_now)[rows, lanes[u]]
                    parts.append(seen[late])
                return jnp.concatenate(parts, axis=1)

            return get

        def back(ref, u, tile):
            return ref[u, :, col(tile)] if tile >= 0 else zero_tile

        def layer0(block_tiles):
            for j in block_tiles:
                shared = base[:, col(j)]
                for u in range(group):
                    inner0[u, :, col(j)] = jnp.maximum(shared + bias_of(u, 0)(j), 0.0).astype(BF16)

        def layer1(u, block_tiles):
            bias = bias_of(u, 1)
            for j in block_tiles:
                rhs = jnp.concatenate(
                    [x_ref[n, 1, :, col(j)], inner0[u, :, col(j)], back(inner0, u, j - 1)], axis=0
                )
                inner1[u, :, col(j)] = jnp.maximum(mm(second, rhs) + bias(j), 0.0).astype(BF16)

        def layer2(u, block_tiles):
            bias = bias_of(u, 2)
            head_bias = bias_full[pl.ds(taps, 1), lanes[u]]
            for j in block_tiles:
                rhs = jnp.concatenate(
                    [
                        x_ref[n, 2, :, col(j)],
                        inner0[u, :, col(j)],
                        back(inner0, u, j - 2),
                        inner1[u, :, col(j)],
                        back(inner1, u, j - 2),
                    ],
                    axis=0,
                )
                v = mm(third, rhs)
                h = jnp.maximum(v[:channels] + bias(j), 0.0) * jnp.concatenate([last, last], axis=1)
                s = (
                    jnp.sum(h, axis=0, keepdims=True)
                    + v[channels : channels + 1]
                    + v[channels + 1 : channels + 2]
                    + jnp.concatenate([head_bias, head_bias], axis=1)
                )
                pred[2 * j, pl.ds(items[u], 1), :] = s[:, :LANES]
                pred[2 * j + 1, pl.ds(items[u], 1), :] = s[:, LANES:]

        blocks = [range(j, min(j + BLOCK, tiles)) for j in range(0, tiles, BLOCK)]
        for step_at in range(len(blocks) + 2):
            if step_at < len(blocks):
                layer0(blocks[step_at])
            for u in range(group):
                if 0 <= step_at - 1 < len(blocks):
                    layer1(u, blocks[step_at - 1])
                if 0 <= step_at - 2 < len(blocks):
                    layer2(u, blocks[step_at - 2])


def net_last(n_crops, *refs):
    x_ref, y_ref, w_ref, pred_first = refs[:4]
    refs = refs[4:]
    preds = [pred_first]
    if n_crops == 2:
        wts, spread = refs[:2]
        out_ref, pred = refs[2:4]
        run_crop(x_ref, 1, wts, spread, pred, *refs[4:])
        preds.append(pred)
    else:
        out_ref = refs[0]
    weeks = y_ref.shape[1]
    members = 2 * pred_first.shape[1]

    lane = lax.broadcasted_iota(jnp.int32, (1, LANES), 1)
    low_half = lane < SLOTS
    region = (lane % SLOTS) // CAP
    masks = [jnp.where(region == r, 1.0, 0.0).astype(BF16) for r in range(REGIONS)]
    gram = jnp.zeros((REGIONS * members, members + 16), F32)
    held = []
    for t in range(weeks):
        scaled, innov = [], []
        for n in range(n_crops):
            p = preds[n][t]
            total = jnp.sum(p, axis=0, keepdims=True)
            mean = (total + pltpu.roll(total, SLOTS, 1)) / members
            w = w_ref[n, pl.ds(t, 1), :]
            y = y_ref[n, pl.ds(t, 1), :]
            scaled.append(w * (p - mean) / math.sqrt(ALPHA_INFLATION * (members - 1)))
            innov.append(w * (y - mean) / math.sqrt(ALPHA_INFLATION))
        if n_crops == 2:
            even = jnp.where(low_half, scaled[0], pltpu.roll(scaled[1], SLOTS, 1))
            odd = jnp.where(low_half, pltpu.roll(scaled[0], SLOTS, 1), scaled[1])
            row = jnp.where(low_half, innov[0], innov[1])
        else:
            even = jnp.where(low_half, scaled[0], 0.0)
            odd = jnp.where(low_half, pltpu.roll(scaled[0], SLOTS, 1), 0.0)
            row = jnp.where(low_half, innov[0], 0.0)
        rows = jnp.concatenate([even, odd], axis=0).astype(BF16)
        high, low = hi_lo(row)
        row_id = lax.broadcasted_iota(jnp.int32, (16, LANES), 0)
        extra = jnp.where(
            row_id == 0, high.astype(F32), jnp.where(row_id == 1, low.astype(F32), 0.0)
        ).astype(BF16)
        masked = jnp.concatenate([rows * mask for mask in masks], axis=0)
        held.append((masked, jnp.concatenate([rows, extra], axis=0)))
        if len(held) == 2:
            gram = gram + mm_nt(
                jnp.concatenate([h[0] for h in held], axis=1),
                jnp.concatenate([h[1] for h in held], axis=1),
            )
            held = []
    flat = jnp.transpose(gram)
    out_ref[...] = flat[: members + 8]


def solve_kernel(owned, gram_a, gram_b, theta_ref, out_ref, system, moved):
    members, _, n_params = theta_ref.shape
    my_members = out_ref.shape[0]
    first_region = lax.axis_index("crop") * owned
    first_member = lax.axis_index("member") * my_members
    gram = gram_a[...] + gram_b[...]
    for r in range(REGIONS):
        system[r] = gram[:, r * members : (r + 1) * members]
    row_id = lax.broadcasted_iota(jnp.int32, (members, 1), 0)
    eye = lax.broadcasted_iota(jnp.int32, (members, members), 0) == lax.broadcasted_iota(
        jnp.int32, (members, members), 1
    )
    scale_root = math.sqrt(members - 1)
    work = []
    for k in range(owned):
        block = system[first_region + k]
        g = block[:members]
        proj = block[members : members + 1] + block[members + 1 : members + 2]
        theta = jnp.concatenate(
            [theta_ref[m, pl.ds(first_region + k, 1), :] for m in range(members)], axis=0
        )
        spread = (theta - jnp.sum(theta, axis=0, keepdims=True) / members) / scale_root
        work.append([g + jnp.where(eye, 1.0, 0.0), spread, proj - scale_root * g, theta])
    for i in range(members):
        for item in work:
            a, z = item[0], item[1]
            column = a[:, i : i + 1]
            pivot = a[i : i + 1, i : i + 1]
            row_a = a[i : i + 1] / pivot
            row_z = z[i : i + 1] / pivot
            factor = jnp.where(row_id == i, column - 1.0, column)
            item[0] = a - factor * row_a
            item[1] = z - factor * row_z
    for k, (_, z, right, theta) in enumerate(work):
        moved[k] = theta + jnp.dot(
            right, z, precision=lax.Precision.HIGHEST, preferred_element_type=F32
        )
    for k in range(owned):
        for m in range(my_members):
            out_ref[m, pl.ds(k, 1), :] = moved[k, pl.ds(first_member + m, 1), :]


def local(
    forcing,
    observed,
    obs_sigma,
    pixel_class,
    pixel_count,
    cloud_free,
    params,
    input_weight,
    conv_weight,
    mix_weight,
    head_weight,
):
    n_crop = lax.axis_size("crop")
    n_member = lax.axis_size("member")
    weeks, n_forcing, pixels = forcing.shape
    local_crops, layers, channels, _ = conv_weight.shape
    my_members, _, n_params = params.shape
    members = my_members * n_member
    assert n_member % local_crops == 0
    split = n_member // local_crops
    dup = max(1, split // n_crop)
    n_crops = max(1, n_crop // split)
    assert n_crops in (1, 2) and n_crops * split == n_crop * dup
    plan = (n_crops, local_crops, split, dup, layers)
    params_kernel = pltpu.CompilerParams(vmem_limit_bytes=VMEM_LIMIT)
    taps, block = weight_rows(layers, channels)
    width = 2 * n_forcing + 2 * (layers - 1) * channels
    assert width % 16 == 0 and width + 2 * channels <= width + 128
    wide = -(-(width + 128 + n_forcing + n_params) // 128) * 128
    vmem_copy = lambda a: pltpu.VMEM(a.shape[1:], a.dtype)

    input_rows = jnp.swapaxes(input_weight, 1, 2)
    folded, theta_own, x, y, w = pl.pallas_call(
        functools.partial(prepare, plan),
        out_shape=(
            jax.ShapeDtypeStruct((block, wide), BF16),
            jax.ShapeDtypeStruct(params.shape, F32),
            jax.ShapeDtypeStruct((n_crops, layers, 2 * n_forcing, weeks * LANES), BF16),
            jax.ShapeDtypeStruct((n_crops, weeks, LANES), F32),
            jax.ShapeDtypeStruct((n_crops, weeks, LANES), F32),
        ),
        in_specs=hbm(11),
        out_specs=tuple(vmem(5)),
        scratch_shapes=[
            vmem_copy(input_rows),
            vmem_copy(conv_weight),
            vmem_copy(mix_weight),
            pltpu.VMEM(head_weight.shape, BF16),
            pltpu.VMEM((weeks * n_forcing, pixels), BF16),
            pltpu.VMEM((weeks, pixels), BF16),
            pltpu.VMEM((1, pixels), F32),
            pltpu.VMEM((1, pixels), jnp.int32),
            pltpu.VMEM(cloud_free.shape, jnp.int32),
            pltpu.SMEM(pixel_count.shape, jnp.int32),
            pltpu.VMEM((2 * channels, width), F32),
            pltpu.VMEM((block, 128), F32),
            pltpu.SemaphoreType.DMA((11,)),
        ],
        compiler_params=params_kernel,
        cost_estimate=cost(2),
    )(
        *stay(
            input_rows,
            conv_weight,
            mix_weight,
            head_weight,
            params,
            forcing.reshape(weeks * n_forcing, pixels),
            observed,
            obs_sigma,
            pixel_class.reshape(1, pixels),
            cloud_free,
            pixel_count,
        )
    )

    if n_crops == n_crop == 2:
        weights = [folded, lax.ppermute(folded, "crop", [(0, 1), (1, 0)])]
    else:
        gathered = lax.all_gather(folded, "crop", axis=0)
        first_j, _ = unit_place(plan, lax.axis_index("member"))
        weights = [
            lax.dynamic_index_in_dim(gathered, unit_crop(plan, n, first_j), 0, keepdims=False)
            for n in range(n_crops)
        ]
    if n_member in (2, 4):
        thetas = [theta_own] + [
            lax.ppermute(params, "member", [(i, i ^ d) for i in range(n_member)])
            for d in range(1, n_member)
        ]
    else:
        thetas = [lax.all_gather(params, "member", axis=0, tiled=True)]

    pairs = members // 2
    group = math.gcd(pairs, GROUP)
    scratch = [
        pltpu.VMEM((channels, weeks * LANES), F32),
        pltpu.VMEM((group, channels, weeks * LANES), BF16),
        pltpu.VMEM((group, channels, weeks * LANES), BF16),
        pltpu.VMEM((block, pairs * LANES), F32),
        pltpu.VMEM((taps, pairs * LANES), F32),
    ]
    pred, theta_all, spread = pl.pallas_call(
        functools.partial(net_first, (len(thetas), n_forcing)),
        out_shape=(
            jax.ShapeDtypeStruct((weeks, pairs, LANES), F32),
            jax.ShapeDtypeStruct((members, REGIONS, n_params), F32),
            jax.ShapeDtypeStruct((pairs * LANES, n_forcing + n_params), F32),
        ),
        in_specs=vmem(2 + len(thetas)),
        out_specs=tuple(vmem(3)),
        scratch_shapes=[pltpu.VMEM((members, REGIONS, n_forcing + n_params), F32)] + scratch,
        compiler_params=params_kernel,
        cost_estimate=cost(7),
    )(x, weights[0], *thetas)
    rest = [x, y, w, pred]
    scratch = [pltpu.VMEM((weeks, pairs, LANES), F32)] + scratch
    if n_crops == 2:
        rest += [weights[1], spread]
    gram = pl.pallas_call(
        functools.partial(net_last, n_crops),
        out_shape=jax.ShapeDtypeStruct((members + 8, REGIONS * members), F32),
        in_specs=vmem(len(rest)),
        out_specs=vmem(1)[0],
        scratch_shapes=scratch if n_crops == 2 else [],
        compiler_params=params_kernel,
        cost_estimate=cost(8),
    )(*rest)

    steps = []
    for axis in ("crop", "pixel", "member"):
        size = lax.axis_size(axis)
        d = 1
        while d < size:
            steps.append((axis, [(i, i ^ d) for i in range(size)]))
            d *= 2
    other = None
    for axis, pairs_ in steps:
        if other is not None:
            gram = gram + other
        other = lax.ppermute(gram, axis, pairs_)

    owned = REGIONS // n_crop
    return pl.pallas_call(
        functools.partial(solve_kernel, owned),
        out_shape=jax.ShapeDtypeStruct((my_members, owned, n_params), F32),
        in_specs=vmem(3),
        out_specs=vmem(1)[0],
        scratch_shapes=[
            pltpu.VMEM((REGIONS, members + 8, members), F32),
            pltpu.VMEM((owned, members, n_params), F32),
        ],
        compiler_params=params_kernel,
        cost_estimate=cost(2),
    )(gram, other, theta_all)


def solution(mesh):
    in_specs = (
        P(None, None, ("pixel", "crop")),
        P(None, ("pixel", "crop")),
        P(("pixel", "crop")),
        P(("pixel", "crop"), None),
        P(("pixel", "crop")),
        P(("pixel", "crop"), None),
        P("member", None, None),
        P("crop", None, None),
        P("crop", None, None, None),
        P("crop", None, None, None),
        P("crop", None),
    )
    out_specs = P("member", "crop", None)
    return jax.shard_map(local, mesh=mesh, in_specs=in_specs, out_specs=out_specs, check_vma=False)
```

```python
import functools
import math

import jax
import jax.numpy as jnp
from jax import lax
from jax.experimental import pallas as pl
from jax.experimental.pallas import tpu as pltpu
from jax.sharding import PartitionSpec as P

REGIONS = 8
CAP = 8
SLOTS = REGIONS * CAP
LANES = 2 * SLOTS
ALPHA_INFLATION = 4.0
GROUP = 4
TURN = 24
VMEM_LIMIT = 48 * 2**20
F32 = jnp.float32
BF16 = jnp.bfloat16

NT = (((1,), (1,)), ((), ()))
TN = (((0,), (0,)), ((), ()))


def mm(a, b):
    return jnp.dot(a, b, preferred_element_type=F32)


def mm_nt(a, b):
    return lax.dot_general(a, b, NT, preferred_element_type=F32)


def hi_lo(x):
    high = x.astype(BF16)
    return high, (x - high.astype(F32)).astype(BF16)


def vmem(n):
    return [pl.BlockSpec(memory_space=pltpu.VMEM)] * n


def hbm(n):
    return [pl.BlockSpec(memory_space=pltpu.HBM)] * n


def cost(microseconds):
    return pl.CostEstimate(
        flops=int(microseconds * 1.1e9), bytes_accessed=int(microseconds * 3.5e6), transcendentals=0
    )


def stay(*arrays):
    return [pltpu.with_memory_space_constraint(a, pltpu.HBM) for a in arrays]


def weight_rows(layers, channels):
    taps = layers * channels
    return taps, taps + 16


def fetch(pairs, sems):
    copies = [pltpu.make_async_copy(src, dst, sems.at[i]) for i, (src, dst) in enumerate(pairs)]
    for copy in copies:
        copy.start()

    def wait():
        for copy in copies:
            copy.wait()

    return wait


def fold_weights(mine, input_ref, conv_ref, mix_ref, head_ref, out_ref, quad, stack):
    layers, channels = conv_ref.shape[0], conv_ref.shape[1]
    forcing = 8
    taps, block = weight_rows(layers, channels)
    out_ref[...] = jnp.zeros(out_ref.shape, BF16)
    quad[...] = jnp.zeros(quad.shape, F32)
    stack[...] = jnp.zeros(stack.shape, F32)
    win = jnp.transpose(input_ref[...].astype(F32))
    for half in range(2):
        rows = pl.ds(half * channels, channels)
        quad[rows, pl.ds(half * forcing, forcing)] = win[:, :forcing]
        for layer in range(layers - 1):
            at = 2 * forcing + (2 * layer + half) * channels
            quad[rows, pl.ds(at, channels)] = mix_ref[layer].astype(F32)
    for layer in range(layers):
        stack[pl.ds(layer * channels, channels), pl.ds(0, 2 * channels)] = conv_ref[layer].astype(
            F32
        )
    head_row = lax.broadcasted_iota(jnp.int32, head_ref.shape, 0)
    head = jnp.sum(
        jnp.where(head_row == mine, head_ref[...].astype(F32), 0.0), axis=0, keepdims=True
    )
    stack[pl.ds(taps, 1), pl.ds(0, channels)] = head
    lhs = stack[:, : 2 * channels].astype(BF16)
    fused = mm(lhs, quad[...].astype(BF16))
    last = mm(lhs[taps:, :channels], mix_ref[layers - 1])
    width = fused.shape[1]
    out_ref[pl.ds(0, taps), pl.ds(0, width)] = fused[:taps].astype(BF16)
    fused_hi, fused_lo = hi_lo(fused[taps : taps + 1])
    last_hi, last_lo = hi_lo(last[:1])
    last_pad = jnp.zeros((2, width - channels), F32)
    last_rows = jnp.concatenate([last_hi.astype(F32), last_lo.astype(F32)], axis=0)
    out_ref[pl.ds(taps, 16), pl.ds(0, width)] = jnp.concatenate(
        [
            fused_hi.astype(F32),
            fused_lo.astype(F32),
            jnp.concatenate([last_rows, last_pad], axis=1),
            jnp.zeros((12, width), F32),
        ],
        axis=0,
    ).astype(BF16)
    out_ref[:, pl.ds(width, 2 * channels)] = lhs
    win = win[:, forcing:]
    win_pad = jnp.zeros((block - channels, win.shape[1]), F32)
    out_ref[:, pl.ds(width + 128, win.shape[1])] = jnp.concatenate([win, win_pad], axis=0).astype(
        BF16
    )


def prepare(plan, *refs):
    sources, refs = refs[:11], refs[11:]
    folded, theta, x, y, w, pred = refs[:6]
    buffers, (quad, stack, sems, spread), scratch = refs[6:16], refs[16:20], refs[20:]
    mine = lax.axis_index("member") // plan[2]
    sliced = [s.at[mine] if i < 3 else s for i, s in enumerate(sources)]
    copies = list(zip(sliced, buffers[:4] + (theta,) + buffers[4:]))
    copies[7] = (copies[7][0], copies[7][1].at[0])
    fetch(copies, sems)()
    fold_weights(mine, *buffers[:4], folded, quad, stack)
    pack_slots(plan, *buffers[4:], x, y, w)
    own = pred.shape[1]
    spread_block(lambda i, r: theta[i, pl.ds(r, 1), :], own, spread, 0)
    run_crop(x, 0, folded, spread, 0, own, lambda i: i, pred, *scratch)


def spread_block(row_of, count, spread, at):
    for i in range(count):
        for half in range(2):
            for r in range(REGIONS):
                row = row_of(i + half * count, r)
                spread[pl.ds((at + i) * LANES + half * SLOTS + r * CAP, CAP), :] = (
                    jnp.broadcast_to(row, (CAP, row.shape[1]))
                )


def pack_slots(
    plan, forcing_ref, observed_ref, sigma_ref, class_ref, cloud_ref, count_ref, x_ref, y_ref, w_ref
):
    n_crops, local_crops, split, dup, layers = plan
    weeks, pixels = observed_ref.shape
    blocks = cloud_ref.shape[0]
    block_len = pixels // blocks
    member = lax.axis_index("member")
    local = member // split
    first_j, part = unit_place(plan, member)
    lane = lax.broadcasted_iota(jnp.int32, (1, pixels), 1)
    live = jnp.zeros((1, pixels), jnp.int32)
    for b in range(blocks):
        here = (lane >= b * block_len) & (lane < b * block_len + count_ref[b])
        live = jnp.where(here, 1, live)
    classes = class_ref[...]
    rank_of = lax.broadcasted_iota(jnp.int32, (CAP, pixels), 0)
    one_hots = []
    for n in range(n_crops):
        crop = unit_crop(plan, n, first_j) * local_crops + local
        one_hots.append(
            jnp.where((classes == crop * REGIONS + rank_of) & (live > 0), 1.0, 0.0).astype(F32)
        )
    hot = jnp.concatenate(one_hots, axis=0)
    if hot.shape[0] < 16:
        hot = jnp.concatenate([hot, jnp.zeros_like(hot)], axis=0)
    earlier = lax.broadcasted_iota(jnp.int32, (pixels, pixels), 0) < lax.broadcasted_iota(
        jnp.int32, (pixels, pixels), 1
    )
    rank = mm(hot.astype(BF16), jnp.where(earlier, 1.0, 0.0).astype(BF16))
    wanted = rank_of.astype(F32)
    if dup > 1:
        wanted = jnp.where(rank_of % dup == part, wanted, -1.0)
    selects = []
    for n in range(n_crops):
        rows = []
        for r in range(REGIONS):
            at = n * REGIONS + r
            match = (rank[at : at + 1] == wanted) & (hot[at : at + 1] > 0)
            rows.append(jnp.where(match, 1.0, 0.0))
        half = jnp.concatenate(rows, axis=0).astype(BF16)
        selects.append(jnp.concatenate([half, half], axis=0))
    select = jnp.concatenate(selects, axis=0)
    block_row = lax.broadcasted_iota(jnp.int32, (blocks, pixels), 0)
    block_lane = lax.broadcasted_iota(jnp.int32, (blocks, pixels), 1)
    in_block = (block_lane >= block_row * block_len) & (block_lane < (block_row + 1) * block_len)
    seen = lax.dot_general(
        cloud_ref[...].astype(F32),
        jnp.where(in_block, 1.0, 0.0),
        TN,
        preferred_element_type=F32,
    )
    weight = (seen / sigma_ref[...]).astype(BF16)
    observed = mm_nt(observed_ref[...], select)
    weight = mm_nt(weight, select)
    packed = mm_nt(forcing_ref[...], select)
    n_forcing = packed.shape[0] // weeks
    zero = jnp.zeros((n_forcing, LANES), F32)
    for n in range(n_crops):
        lanes = slice(n * LANES, (n + 1) * LANES)
        y_ref[n] = observed[:, lanes]
        w_ref[n] = weight[:, lanes]
        for t in range(weeks):
            now = packed[t * n_forcing : (t + 1) * n_forcing, lanes]
            for layer in range(layers):
                back = t - 2**layer
                then = packed[back * n_forcing : (back + 1) * n_forcing, lanes] if back >= 0 else zero
                x_ref[n, layer, :, pl.ds(t * LANES, LANES)] = jnp.concatenate(
                    [now, then], axis=0
                ).astype(BF16)


def unit_place(plan, member):
    n_crops, _, split, dup, _ = plan
    step = lax.rem(member, split)
    return (step // dup) * n_crops, lax.rem(step, dup)


def unit_crop(plan, n, first_j):
    return lax.rem(first_j + n + swap_base(plan), plan_shards(plan))


def swap_base(plan):
    return lax.axis_index("crop") if plan[0] == plan_shards(plan) else 0


def plan_shards(plan):
    return lax.axis_size("crop")


def other_member(d):
    me, count = lax.axis_index("member"), lax.axis_size("member")
    return me ^ d if count in (2, 4) else lax.rem(me + d, count)


def pair_row(i, own):
    return other_member(lax.div(i, own)) * own + lax.rem(i, own)


def net_first(blocks_in, *refs):
    x_ref, wts, pred_own, theta_own = refs[:4]
    theta_refs, refs = refs[4 : 4 + blocks_in], refs[4 + blocks_in :]
    pred, theta_out, spread = refs[:3]
    scratch = refs[3:]
    block = theta_own.shape[0]
    own = block // 2
    shards = theta_out.shape[0] // block
    weeks, pairs = pred.shape[0], pred.shape[1]
    me = lax.axis_index("member")

    for i in range(block):
        theta_out[me * block + i] = theta_own[i]
    spread_block(lambda i, r: theta_own[i, pl.ds(r, 1), :], own, spread, 0)
    for d in range(1, shards):
        if blocks_in == 1 and shards > 2:
            ref, at = theta_refs[0], other_member(d) * block
        else:
            ref, at = theta_refs[d - 1], 0
        for i in range(block):
            theta_out[other_member(d) * block + i] = ref[at + i]
        spread_block(lambda i, r: ref[at + i, pl.ds(r, 1), :], own, spread, d * own)
    for t in range(weeks):
        for i in range(own):
            pred[t, pl.ds(me * own + i, 1), :] = pred_own[t, pl.ds(i, 1), :]
    run_crop(
        x_ref, 0, wts, spread, own, pairs - own, lambda i: pair_row(i + own, own), pred, *scratch
    )


def run_crop(
    x_ref, n, wts, spread, start, pairs, row_of, pred, base, inner0, inner1, bias_full, bias_now
):
    layers, n_forcing = x_ref.shape[1], x_ref.shape[2] // 2
    channels = base.shape[0]
    taps, block = weight_rows(layers, channels)
    width = 2 * n_forcing + 2 * (layers - 1) * channels
    tiles = pred.shape[0] // 2
    span = 2 * LANES

    def col(j):
        return pl.ds(j * span, span)

    stack = wts[:, pl.ds(width, 2 * channels)]
    now = stack[:taps, :channels]
    win = wts[pl.ds(0, channels), pl.ds(width + 128, spread.shape[1])]
    theta_rows = spread[pl.ds(start * LANES, pairs * LANES), :].astype(BF16)
    high, low = hi_lo(mm_nt(win, theta_rows))
    bias_full[...] = mm(
        jnp.concatenate([stack, stack], axis=1),
        jnp.concatenate([high, high, low, low], axis=0),
    )
    bias_now[...] = mm(
        jnp.concatenate([now, now], axis=1), jnp.concatenate([high, low], axis=0)
    )
    tail = wts[pl.ds(taps, 16), pl.ds(0, channels)].astype(F32)
    tail_row = tail[2:3] + tail[3:4]
    diag = lax.broadcasted_iota(jnp.int32, (channels, channels), 0) == lax.broadcasted_iota(
        jnp.int32, (channels, channels), 1
    )
    tail_col = jnp.sum(jnp.where(diag, tail_row, 0.0), axis=1, keepdims=True)
    last = jnp.broadcast_to(tail_col, (channels, LANES))
    first = wts[pl.ds(0, channels), pl.ds(0, 2 * n_forcing)]
    base[...] = mm(first, x_ref[n, 0])
    second = wts[pl.ds(channels, channels), pl.ds(0, 2 * n_forcing + 2 * channels)]
    third = wts[pl.ds(2 * channels, channels + 16), pl.ds(0, width)]
    zero_tile = jnp.zeros((channels, span), BF16)

    group = inner0.shape[0]
    length = TURN // group

    @pl.loop(0, pairs // group)
    def _(step):
        items = [step * group + u for u in range(group)]
        rows_out = [row_of(i) for i in items]
        lanes = [pl.ds(pl.multiple_of(i * LANES, LANES), LANES) for i in items]

        def bias_of(u, layer):
            rows = pl.ds(layer * channels, channels)
            seen = {}

            def get(tile):
                parts = []
                for t in (2 * tile, 2 * tile + 1):
                    late = t >= 2**layer
                    if late not in seen:
                        seen[late] = (bias_full if late else bias_now)[rows, lanes[u]]
                    parts.append(seen[late])
                return jnp.concatenate(parts, axis=1)

            return get

        def back(ref, u, tile):
            return ref[u, :, col(tile)] if tile >= 0 else zero_tile

        def layer0(block_tiles):
            for j in block_tiles:
                shared = base[:, col(j)]
                for u in range(group):
                    inner0[u, :, col(j)] = jnp.maximum(shared + bias_of(u, 0)(j), 0.0).astype(BF16)

        def layer1(u, block_tiles):
            bias = bias_of(u, 1)
            for j in block_tiles:
                rhs = jnp.concatenate(
                    [x_ref[n, 1, :, col(j)], inner0[u, :, col(j)], back(inner0, u, j - 1)], axis=0
                )
                inner1[u, :, col(j)] = jnp.maximum(mm(second, rhs) + bias(j), 0.0).astype(BF16)

        def layer2(u, block_tiles):
            bias = bias_of(u, 2)
            head_bias = bias_full[pl.ds(taps, 1), lanes[u]]
            for j in block_tiles:
                rhs = jnp.concatenate(
                    [
                        x_ref[n, 2, :, col(j)],
                        inner0[u, :, col(j)],
                        back(inner0, u, j - 2),
                        inner1[u, :, col(j)],
                        back(inner1, u, j - 2),
                    ],
                    axis=0,
                )
                v = mm(third, rhs)
                h = jnp.maximum(v[:channels] + bias(j), 0.0) * jnp.concatenate([last, last], axis=1)
                s = (
                    jnp.sum(h, axis=0, keepdims=True)
                    + v[channels : channels + 1]
                    + v[channels + 1 : channels + 2]
                    + jnp.concatenate([head_bias, head_bias], axis=1)
                )
                pred[2 * j, pl.ds(rows_out[u], 1), :] = s[:, :LANES]
                pred[2 * j + 1, pl.ds(rows_out[u], 1), :] = s[:, LANES:]

        blocks = [range(j, min(j + length, tiles)) for j in range(0, tiles, length)]
        for step_at in range(len(blocks) + 2):
            if step_at < len(blocks):
                layer0(blocks[step_at])
            for u in range(group):
                if 0 <= step_at - 1 < len(blocks):
                    layer1(u, blocks[step_at - 1])
                if 0 <= step_at - 2 < len(blocks):
                    layer2(u, blocks[step_at - 2])


def net_last(n_crops, own, *refs):
    x_ref, y_ref, w_ref, pred_first = refs[:4]
    refs = refs[4:]
    preds = [pred_first]
    if n_crops == 2:
        wts, spread = refs[:2]
        out_ref, pred = refs[2:4]
        run_crop(
            x_ref, 1, wts, spread, 0, pred.shape[1], lambda i: pair_row(i, own), pred, *refs[4:]
        )
        preds.append(pred)
    else:
        out_ref = refs[0]
    weeks = y_ref.shape[1]
    members = 2 * pred_first.shape[1]

    lane = lax.broadcasted_iota(jnp.int32, (1, LANES), 1)
    low_half = lane < SLOTS
    region = (lane % SLOTS) // CAP
    masks = [jnp.where(region == r, 1.0, 0.0).astype(BF16) for r in range(REGIONS)]
    gram = jnp.zeros((REGIONS * members, members + 16), F32)
    held = []
    for t in range(weeks):
        scaled, innov = [], []
        for n in range(n_crops):
            p = preds[n][t]
            total = jnp.sum(p, axis=0, keepdims=True)
            mean = (total + pltpu.roll(total, SLOTS, 1)) / members
            w = w_ref[n, pl.ds(t, 1), :]
            y = y_ref[n, pl.ds(t, 1), :]
            scaled.append(w * (p - mean) / math.sqrt(ALPHA_INFLATION * (members - 1)))
            innov.append(w * (y - mean) / math.sqrt(ALPHA_INFLATION))
        if n_crops == 2:
            even = jnp.where(low_half, scaled[0], pltpu.roll(scaled[1], SLOTS, 1))
            odd = jnp.where(low_half, pltpu.roll(scaled[0], SLOTS, 1), scaled[1])
            row = jnp.where(low_half, innov[0], innov[1])
        else:
            even = jnp.where(low_half, scaled[0], 0.0)
            odd = jnp.where(low_half, pltpu.roll(scaled[0], SLOTS, 1), 0.0)
            row = jnp.where(low_half, innov[0], 0.0)
        rows = jnp.concatenate([even, odd], axis=0).astype(BF16)
        high, low = hi_lo(row)
        row_id = lax.broadcasted_iota(jnp.int32, (16, LANES), 0)
        extra = jnp.where(
            row_id == 0, high.astype(F32), jnp.where(row_id == 1, low.astype(F32), 0.0)
        ).astype(BF16)
        masked = jnp.concatenate([rows * mask for mask in masks], axis=0)
        held.append((masked, jnp.concatenate([rows, extra], axis=0)))
        if len(held) == 2:
            gram = gram + mm_nt(
                jnp.concatenate([h[0] for h in held], axis=1),
                jnp.concatenate([h[1] for h in held], axis=1),
            )
            held = []
    flat = jnp.transpose(gram)
    out_ref[...] = flat[: members + 8]


def solve_kernel(owned, gram_a, gram_b, theta_ref, out_ref, system, moved, joint):
    members, _, n_params = theta_ref.shape
    my_members = out_ref.shape[0]
    own, pairs = my_members // 2, members // 2
    order = [p // own * my_members + p % own + half * own for half in range(2) for p in range(pairs)]
    first_region = lax.axis_index("crop") * owned
    first_pair = lax.axis_index("member") * own
    gram = gram_a[...] + gram_b[...]
    for r in range(REGIONS):
        system[r] = gram[:, r * members : (r + 1) * members]
    row_id = lax.broadcasted_iota(jnp.int32, (members, 1), 0)
    eye = lax.broadcasted_iota(jnp.int32, (members, members), 0) == lax.broadcasted_iota(
        jnp.int32, (members, members), 1
    )
    scale_root = math.sqrt(members - 1)
    joint[...] = jnp.zeros(joint.shape, F32)
    work = []
    for k in range(owned):
        block = system[first_region + k]
        g = block[:members]
        proj = block[members : members + 1] + block[members + 1 : members + 2]
        theta = jnp.concatenate(
            [theta_ref[m, pl.ds(first_region + k, 1), :] for m in order], axis=0
        )
        spread = (theta - jnp.sum(theta, axis=0, keepdims=True) / members) / scale_root
        joint[k, :, pl.ds(0, members)] = g + jnp.where(eye, 1.0, 0.0)
        joint[k, :, pl.ds(members, n_params)] = spread
        work.append((proj - scale_root * g, theta))
    both = [joint[k] for k in range(owned)]
    width = joint.shape[2]
    for i in range(0, members, 2):
        for k, a in enumerate(both):
            col0 = jnp.broadcast_to(a[:, i : i + 1], (members, width))
            col1 = jnp.broadcast_to(a[:, i + 1 : i + 2], (members, width))
            inv0 = 1.0 / col0[i : i + 1]
            row0 = a[i : i + 1] * inv0
            below = col0[i + 1 : i + 2]
            ahead = col1[i : i + 1] * inv0
            inv1 = 1.0 / (col1[i + 1 : i + 2] - below * ahead)
            row1 = (a[i + 1 : i + 2] - below * row0) * inv1
            row0 = row0 - ahead * row1
            col0 = jnp.where(row_id == i, col0 - 1.0, col0)
            col1 = jnp.where(row_id == i + 1, col1 - 1.0, col1)
            both[k] = a - col0 * row0 - col1 * row1
    for k, (right, theta) in enumerate(work):
        joint[k] = both[k]
        z = joint[k, :, pl.ds(members, n_params)]
        moved[k] = theta + jnp.dot(
            right, z, precision=lax.Precision.HIGHEST, preferred_element_type=F32
        )
    for k in range(owned):
        for m in range(my_members):
            row = first_pair + m // own * pairs + m % own
            out_ref[m, pl.ds(k, 1), :] = moved[k, pl.ds(row, 1), :]


def local(
    forcing,
    observed,
    obs_sigma,
    pixel_class,
    pixel_count,
    cloud_free,
    params,
    input_weight,
    conv_weight,
    mix_weight,
    head_weight,
):
    n_crop = lax.axis_size("crop")
    n_member = lax.axis_size("member")
    weeks, n_forcing, pixels = forcing.shape
    local_crops, layers, channels, _ = conv_weight.shape
    my_members, _, n_params = params.shape
    members = my_members * n_member
    assert n_member % local_crops == 0
    split = n_member // local_crops
    dup = max(1, split // n_crop)
    n_crops = max(1, n_crop // split)
    assert n_crops in (1, 2) and n_crops * split == n_crop * dup
    plan = (n_crops, local_crops, split, dup, layers)
    params_kernel = pltpu.CompilerParams(vmem_limit_bytes=VMEM_LIMIT)
    taps, block = weight_rows(layers, channels)
    width = 2 * n_forcing + 2 * (layers - 1) * channels
    assert width % 16 == 0 and width + 2 * channels <= width + 128
    wide = -(-(width + 128 + n_forcing + n_params) // 128) * 128
    vmem_copy = lambda a: pltpu.VMEM(a.shape[1:], a.dtype)

    own, pairs = my_members // 2, members // 2

    def scratch(count):
        group = max(g for g in range(1, GROUP + 1) if count % g == 0)
        return [
            pltpu.VMEM((channels, weeks * LANES), F32),
            pltpu.VMEM((group, channels, weeks * LANES), BF16),
            pltpu.VMEM((group, channels, weeks * LANES), BF16),
            pltpu.VMEM((block, count * LANES), F32),
            pltpu.VMEM((taps, count * LANES), F32),
        ]

    input_rows = jnp.swapaxes(input_weight, 1, 2)
    folded, theta_own, x, y, w, pred_own = pl.pallas_call(
        functools.partial(prepare, plan),
        out_shape=(
            jax.ShapeDtypeStruct((block, wide), BF16),
            jax.ShapeDtypeStruct(params.shape, F32),
            jax.ShapeDtypeStruct((n_crops, layers, 2 * n_forcing, weeks * LANES), BF16),
            jax.ShapeDtypeStruct((n_crops, weeks, LANES), F32),
            jax.ShapeDtypeStruct((n_crops, weeks, LANES), F32),
            jax.ShapeDtypeStruct((weeks, own, LANES), F32),
        ),
        in_specs=hbm(11),
        out_specs=tuple(vmem(6)),
        scratch_shapes=[
            vmem_copy(input_rows),
            vmem_copy(conv_weight),
            vmem_copy(mix_weight),
            pltpu.VMEM(head_weight.shape, BF16),
            pltpu.VMEM((weeks * n_forcing, pixels), BF16),
            pltpu.VMEM((weeks, pixels), BF16),
            pltpu.VMEM((1, pixels), F32),
            pltpu.VMEM((1, pixels), jnp.int32),
            pltpu.VMEM(cloud_free.shape, jnp.int32),
            pltpu.SMEM(pixel_count.shape, jnp.int32),
            pltpu.VMEM((2 * channels, width), F32),
            pltpu.VMEM((block, 128), F32),
            pltpu.SemaphoreType.DMA((11,)),
            pltpu.VMEM((own * LANES, n_params), F32),
        ]
        + scratch(own),
        compiler_params=params_kernel,
        cost_estimate=cost(4),
    )(
        *stay(
            input_rows,
            conv_weight,
            mix_weight,
            head_weight,
            params,
            forcing.reshape(weeks * n_forcing, pixels),
            observed,
            obs_sigma,
            pixel_class.reshape(1, pixels),
            cloud_free,
            pixel_count,
        )
    )

    if n_crops == n_crop == 2:
        weights = [folded, lax.ppermute(folded, "crop", [(0, 1), (1, 0)])]
    else:
        gathered = lax.all_gather(folded, "crop", axis=0)
        first_j, _ = unit_place(plan, lax.axis_index("member"))
        weights = [
            lax.dynamic_index_in_dim(gathered, unit_crop(plan, n, first_j), 0, keepdims=False)
            for n in range(n_crops)
        ]
    if n_member in (2, 4):
        thetas = [
            lax.ppermute(params, "member", [(i, i ^ d) for i in range(n_member)])
            for d in range(1, n_member)
        ]
    else:
        thetas = [lax.all_gather(params, "member", axis=0, tiled=True)]

    pred, theta_all, spread = pl.pallas_call(
        functools.partial(net_first, len(thetas)),
        out_shape=(
            jax.ShapeDtypeStruct((weeks, pairs, LANES), F32),
            jax.ShapeDtypeStruct((members, REGIONS, n_params), F32),
            jax.ShapeDtypeStruct((pairs * LANES, n_params), F32),
        ),
        in_specs=vmem(4 + len(thetas)),
        out_specs=tuple(vmem(3)),
        scratch_shapes=scratch(pairs - own),
        compiler_params=params_kernel,
        cost_estimate=cost(5),
    )(x, weights[0], pred_own, theta_own, *thetas)
    rest = [x, y, w, pred]
    held = []
    if n_crops == 2:
        rest += [weights[1], spread]
        held = [pltpu.VMEM((weeks, pairs, LANES), F32)] + scratch(pairs)
    gram = pl.pallas_call(
        functools.partial(net_last, n_crops, own),
        out_shape=jax.ShapeDtypeStruct((members + 8, REGIONS * members), F32),
        in_specs=vmem(len(rest)),
        out_specs=vmem(1)[0],
        scratch_shapes=held,
        compiler_params=params_kernel,
        cost_estimate=cost(7),
    )(*rest)

    steps = []
    for axis in ("crop", "pixel", "member"):
        size = lax.axis_size(axis)
        d = 1
        while d < size:
            steps.append((axis, [(i, i ^ d) for i in range(size)]))
            d *= 2
    other = None
    for axis, pairs_ in steps:
        if other is not None:
            gram = gram + other
        other = lax.ppermute(gram, axis, pairs_)

    owned = REGIONS // n_crop
    return pl.pallas_call(
        functools.partial(solve_kernel, owned),
        out_shape=jax.ShapeDtypeStruct((my_members, owned, n_params), F32),
        in_specs=vmem(3),
        out_specs=vmem(1)[0],
        scratch_shapes=[
            pltpu.VMEM((REGIONS, members + 8, members), F32),
            pltpu.VMEM((owned, members, n_params), F32),
            pltpu.VMEM((owned, members, -(-(members + n_params) // 128) * 128), F32),
        ],
        compiler_params=params_kernel,
        cost_estimate=cost(2),
    )(gram, other, theta_all)


def solution(mesh):
    in_specs = (
        P(None, None, ("pixel", "crop")),
        P(None, ("pixel", "crop")),
        P(("pixel", "crop")),
        P(("pixel", "crop"), None),
        P(("pixel", "crop")),
        P(("pixel", "crop"), None),
        P("member", None, None),
        P("crop", None, None),
        P("crop", None, None, None),
        P("crop", None, None, None),
        P("crop", None),
    )
    out_specs = P("member", "crop", None)
    return jax.shard_map(local, mesh=mesh, in_specs=in_specs, out_specs=out_specs, check_vma=False)
```
